32 devices in a mesh: dp: 16 (over z, x, core), tensor: 2 (over y).
Axes of the slice: x: 2, y: 2, z: 4, core: 2. Of those that a mesh axis runs over, the one named last changes fastest.
Arguments:
- grads: bfloat16 [32, 1024, 1024], P(None, 'dp', 'tensor'), may hold values from -63 to 63
- momentum: float32 [32, 1024, 1024], P(None, 'dp', 'tensor'), may hold values from -63 to 63
- left_root: bfloat16 [48, 1024, 1024], P('dp', 'tensor'), may hold values from -3.5 to 3.5
- right_root: bfloat16 [48, 1024, 1024], P('dp', 'tensor'), may hold values from -3.5 to 3.5
- assign_list: int32 [32], replicated, may hold values from 0 to 31, each once
- owner_counts: int32 [16], replicated, may hold values from 1 to 3, 32 in all
Outputs:
- moment_out: float32 [32, 1024, 1024], P(None, 'dp', 'tensor')
- update: bfloat16 [32, 1024, 1024], P(None, 'dp', 'tensor')
The draws below stay inside these ranges and needn't reach their ends.
Inputs may be any that keep to these rules, and one draw needn't show every extreme that they name: owner_counts sum to 32; the largest is 3.
All inputs are finite; a program needn't handle non-finite values.
Results may differ from the reference program's by a relative error of at most 0.0057.
Values may be sent and summed in bfloat16 or wider, within the bound.
No kernel may reach another device: no remote copies, remote signals or barrier semaphores. Data moves between devices by JAX's collectives and lax.ppermute only.
A program may use at most 128 MiB of HBM per device.

```python
import math
import jax
import jax.numpy as jnp
import numpy as np
from jax import lax

B = 1024
NB = 32
CAP = 3
N_DP = 16


def draw_grads(key, part):
    key = jax.random.fold_in(key, 11)
    knoise, krows, kcols = jax.random.split(key, 3)
    rise = 3.0 ** (jnp.arange(B, dtype=jnp.float32) / B)
    rows = 10.0 ** jax.random.uniform(krows, (NB, B, 1)) * rise[None, :, None]
    cols = 10.0 ** jax.random.uniform(kcols, (NB, 1, B))
    noise = jax.random.normal(knoise, (NB, B, B))
    noise = jnp.clip(noise, -5.0, 5.0)
    return (noise * rows * cols / 24.0).astype(jnp.bfloat16)


def draw_momentum(key, part):
    key = jax.random.fold_in(key, 13)
    knoise, krows, kcols = jax.random.split(key, 3)
    rise = 3.0 ** (jnp.arange(B, dtype=jnp.float32) / B)
    rows = 10.0 ** jax.random.uniform(krows, (NB, B, 1)) * rise[None, :, None]
    cols = 10.0 ** jax.random.uniform(kcols, (NB, 1, B))
    noise = jax.random.normal(knoise, (NB, B, B))
    noise = jnp.clip(noise, -5.0, 5.0)
    return (noise * rows * cols / 24.0).astype(jnp.float32)


def root_matrix(kdiag, koff, low):
    diag = low + jax.random.uniform(kdiag, (N_DP * CAP, B))
    raw = jnp.clip(jax.random.normal(koff, (N_DP * CAP, B, B)), -5.0, 5.0)
    off = (raw + jnp.swapaxes(raw, 1, 2)) * (0.35 / jnp.sqrt(float(B)))
    eye = (jnp.arange(B)[:, None] == jnp.arange(B)[None, :]).astype(jnp.float32)
    return off * (1.0 - eye) + eye * diag[:, :, None]


def draw_left_root(key, part):
    key = jax.random.fold_in(key, 21)
    kdiag, koff = jax.random.split(key, 2)
    matrix = root_matrix(kdiag, koff, 0.5)
    return matrix.astype(jnp.bfloat16)


def draw_right_root(key, part):
    key = jax.random.fold_in(key, 23)
    kdiag, koff = jax.random.split(key, 2)
    matrix = root_matrix(kdiag, koff, 0.5)
    return matrix.astype(jnp.bfloat16)


def length_profile(amount, total, bound, slope):
    weights = [(1 << 20) // math.isqrt(standing ** slope) + 1 for standing in range(2, amount + 1)]
    surplus, given = total - bound - (amount - 1), [1] * (amount - 1)
    while surplus > 0:
        free = [i for i in range(amount - 1) if given[i] < bound]
        whole, left = sum([weights[i] for i in free]), surplus
        for i in free:
            more = min(bound - given[i], max(1, left * weights[i] // whole), surplus)
            given[i] = given[i] + more
            surplus = surplus - more
    return np.array([bound] + given)


def uneven(key, count, total, bound, skew):
    if count == 2:
        one = jax.random.randint(key, (), max(1, total - bound), min(bound, total - 1) + 1)
        return jnp.stack([one, total - one])
    tallies = jnp.asarray(length_profile(count, total, bound, skew), jnp.int32)
    couples = (count - 1) // 2
    giver, receiver = tallies[1:1 + 2 * couples:2], tallies[2:2 + 2 * couples:2]
    slack = jnp.minimum(giver - 1, bound - receiver)
    passed = jax.random.randint(jax.random.fold_in(key, 1), (couples,), 0, 1 << 20) % (slack + 1)
    tallies = tallies.at[1:1 + 2 * couples:2].set(giver - passed).at[2:2 + 2 * couples:2].set(receiver + passed)
    return tallies[jax.random.permutation(jax.random.fold_in(key, 2), count)]


def setup_inputs(seed: int = 0) -> dict:
    keys = jax.random.split(jax.random.key(seed), 7)
    grads = draw_grads(jax.random.fold_in(keys[6], 71), 0)
    momentum = draw_momentum(jax.random.fold_in(keys[6], 71), 0)
    left_root = draw_left_root(jax.random.fold_in(keys[6], 71), 0)
    right_root = draw_right_root(jax.random.fold_in(keys[6], 71), 0)
    assign_list = jax.random.permutation(keys[4], NB).astype(jnp.int32)
    owner_counts = uneven(keys[5], N_DP, NB, CAP, 2).astype(jnp.int32)
    return {"grads": grads, "momentum": momentum, "left_root": left_root, "right_root": right_root, "assign_list": assign_list, "owner_counts": owner_counts}


BETA = 0.9
EPS = 1e-06

def tables(assign_list, owner_counts, cap):
    blocks = assign_list.shape[0]
    offsets = (jnp.cumsum(owner_counts) - owner_counts).astype(jnp.int32)
    slot_ids = jnp.arange(cap, dtype=jnp.int32)
    where_at = offsets[:, None] + slot_ids[None, :]
    live = slot_ids[None, :] < owner_counts[:, None]
    picked = assign_list[jnp.clip(where_at, 0, blocks - 1)]
    slot_block = jnp.where(live, picked, -1).reshape(-1).astype(jnp.int32)
    position = jnp.zeros((blocks,), jnp.int32).at[assign_list].set(jnp.arange(blocks, dtype=jnp.int32))
    owner_of = (lax.optimization_barrier(jnp.sum((offsets[None, :] <= position[:, None]).astype(jnp.int32), axis=1)) - 1).astype(jnp.int32)
    block_slot = (owner_of * cap + position - offsets[owner_of]).astype(jnp.int32)
    return (slot_block, block_slot)

def reference(grads, momentum, left_root, right_root, assign_list, owner_counts):
    moment_out = BETA * momentum + (1.0 - BETA) * grads.astype(jnp.float32)
    slot_block, block_slot = tables(assign_list, owner_counts, CAP)

    def one_block(items):
        moment, index = items
        moment_half = moment.astype(jnp.bfloat16)
        left = left_root[index]
        right = right_root[index]
        product = jnp.dot(moment_half, right.T, preferred_element_type=jnp.float32).astype(jnp.bfloat16)
        direction = jnp.dot(left, product, preferred_element_type=jnp.float32)
        scale = jnp.sqrt(jnp.mean(moment * moment) + EPS) / jnp.sqrt(jnp.mean(direction * direction) + EPS)
        return (direction * scale).astype(jnp.bfloat16)
    update = lax.map(one_block, (moment_out, block_slot))
    return (moment_out, update)
```

```python
import functools

import jax
import jax.numpy as jnp
from jax import lax
from jax.experimental import pallas as pl
from jax.experimental.pallas import tpu as pltpu
from jax.sharding import PartitionSpec as P

BETA = 0.9
EPS = 1e-06
MIB = 1 << 20


def tables(assign_list, owner_counts, cap):
    blocks, owners = assign_list.shape[0], owner_counts.shape[0]
    before = jnp.arange(owners)[None, :] < jnp.arange(owners)[:, None]
    offsets = jnp.sum(jnp.where(before, owner_counts[None, :], 0), axis=1)
    slots = jnp.arange(cap, dtype=jnp.int32)
    where_at = offsets[None, :] + slots[:, None]
    live = slots[:, None] < owner_counts[None, :]
    hit = (where_at[:, :, None] == jnp.arange(blocks)) & live[:, :, None]
    slot_block = jnp.sum(jnp.where(hit, assign_list, 0), axis=2)
    mine = (slot_block[:, :, None] == jnp.arange(blocks)) & live[:, :, None]
    place = jnp.arange(cap * owners, dtype=jnp.int32).reshape(cap, owners, 1)
    block_place = jnp.sum(jnp.where(mine, place, 0), axis=(0, 1))
    return slot_block, block_place


def root_kernel(parts, turn_ref, *refs):
    moments, right, lefts = refs[:parts], refs[parts], refs[parts + 1 : 2 * parts + 1]
    out_ref, square_ref, product = refs[2 * parts + 1 :]
    order, width = moments[0].shape
    step = min(256, order)
    turn = turn_ref[0]

    def places(d):
        at = lax.rem(turn - d + parts, parts) * width
        return pl.multiple_of(at, width)

    def first(i, carry):
        rows = pl.ds(pl.multiple_of(i * step, step), step)
        total = None
        for d in range(parts):
            term = lax.dot_general(
                moments[d][rows, :],
                right[0, :, pl.ds(places(d), width)],
                (((1,), (1,)), ((), ())),
                preferred_element_type=jnp.float32,
            )
            total = term if total is None else total + term
        product[rows, :] = total.astype(jnp.bfloat16)
        return carry

    lax.fori_loop(0, order // step, first, 0)
    small = min(256, width)
    squares = jnp.zeros((1, product.shape[1]), jnp.float32)
    for d in range(parts):
        def second(i, squares, d=d):
            at = pl.multiple_of(i * small, small)
            left = lefts[d][0, pl.ds(at, small), :] if d == 0 else lefts[d][pl.ds(at, small), :]
            direction = jnp.dot(left, product[...], preferred_element_type=jnp.float32)
            rows = pl.ds(pl.multiple_of(places(d) + at, small), small)
            out_ref[rows, :] = direction.astype(jnp.bfloat16)
            return squares + jnp.sum(direction * direction, axis=0, keepdims=True)

        squares = lax.fori_loop(0, width // small, second, squares)
    square_ref[...] = squares


def precondition(slot, turn, moments, right_root, left_root, lefts):
    parts = len(moments)
    order, width = moments[0].shape
    whole = pl.BlockSpec((order, width), lambda i, t: (0, 0))
    piece = pl.BlockSpec((width, order), lambda i, t: (0, 0))
    picked = pl.BlockSpec((1, width, order), lambda i, t: (slot, 0, 0))
    return pl.pallas_call(
        functools.partial(root_kernel, parts),
        grid_spec=pltpu.PrefetchScalarGridSpec(
            num_scalar_prefetch=1,
            grid=(1,),
            in_specs=[whole] * parts + [picked, picked] + [piece] * (parts - 1),
            out_specs=[whole, pl.BlockSpec((1, width), lambda i, t: (0, 0))],
            scratch_shapes=[pltpu.VMEM((order, width), jnp.bfloat16)],
        ),
        out_shape=[
            jax.ShapeDtypeStruct((order, width), jnp.bfloat16),
            jax.ShapeDtypeStruct((1, width), jnp.float32),
        ],
        compiler_params=pltpu.CompilerParams(vmem_limit_bytes=40 * MIB),
        cost_estimate=pl.CostEstimate(
            flops=4 * order * order * width, bytes_accessed=12 * order * width, transcendentals=0
        ),
    )(turn, *moments, right_root, left_root, *lefts)


def finish_kernel(place_ref, scale_ref, *refs):
    slots, out_ref = refs[:-1], refs[-1]
    owners = slots[0].shape[0]

    def one(b, carry):
        place = place_ref[b]
        scale = scale_ref[b]
        for s, slot in enumerate(slots):
            @pl.when(place // owners == s)
            def _(slot=slot, s=s):
                value = slot[place - s * owners].astype(jnp.float32) * scale
                out_ref[b] = value.astype(jnp.bfloat16)
        return carry

    lax.fori_loop(0, out_ref.shape[0], one, 0)


def finish(block_place, scale, arrived):
    owners, rows, columns = arrived[0].shape
    blocks = block_place.shape[0]
    full = pl.BlockSpec((owners, rows, columns), lambda i, *_: (0, 0, 0))
    return pl.pallas_call(
        finish_kernel,
        grid_spec=pltpu.PrefetchScalarGridSpec(
            num_scalar_prefetch=2,
            grid=(1,),
            in_specs=[full] * len(arrived),
            out_specs=pl.BlockSpec((blocks, rows, columns), lambda i, *_: (0, 0, 0)),
        ),
        out_shape=jax.ShapeDtypeStruct((blocks, rows, columns), jnp.bfloat16),
        compiler_params=pltpu.CompilerParams(vmem_limit_bytes=40 * MIB),
    )(block_place, scale, *arrived)


def body(parts, grads, momentum, left_root, right_root, assign_list, owner_counts):
    cap, width, order = left_root.shape
    owners = owner_counts.shape[0]
    cells = float(order * order)
    turn = lax.axis_index("tensor").astype(jnp.int32).reshape(1)
    me = lax.axis_index("dp")

    def around(x):
        return [
            lax.ppermute(x, "tensor", [(s, (s + d) % parts) for s in range(parts)])
            for d in range(1, parts)
        ]

    slot_block, block_place = tables(assign_list, owner_counts, cap)
    moment_out = BETA * momentum + (1.0 - BETA) * grads.astype(jnp.float32)
    moment_half = moment_out.astype(jnp.bfloat16)
    squares = jnp.sum(moment_out * moment_out, axis=(1, 2))

    lefts = [around(left_root[s]) for s in range(cap)]
    arrived, direction_squares = [], []
    for s in range(cap):
        outgoing = moment_half[slot_block[s]]
        columns = lax.all_to_all(outgoing, "dp", split_axis=0, concat_axis=0, tiled=True)
        columns = columns.reshape(order, width)
        direction, square = precondition(
            s, turn, [columns] + around(columns), right_root, left_root, lefts[s]
        )
        direction_squares.append(jnp.sum(square))
        direction = direction.reshape(owners, order // owners, width)
        arrived.append(lax.all_to_all(direction, "dp", split_axis=0, concat_axis=0, tiled=True))
    own = jnp.where(jnp.arange(owners)[None, :] == me, jnp.stack(direction_squares)[:, None], 0.0)
    sums = lax.psum(jnp.concatenate([squares, own.reshape(-1)]), ("dp", "tensor"))
    blocks = squares.shape[0]
    owned = sums[blocks:][block_place]
    scale = jnp.sqrt(sums[:blocks] / cells + EPS) / jnp.sqrt(owned / cells + EPS)
    return (moment_out, finish(block_place, scale, arrived))


def solution(mesh):
    parts = mesh.shape["tensor"]
    in_specs = (
        P(None, "dp", "tensor"),
        P(None, "dp", "tensor"),
        P("dp", "tensor", None),
        P("dp", "tensor", None),
        P(),
        P(),
    )
    out_specs = (P(None, "dp", "tensor"), P(None, "dp", "tensor"))
    return jax.shard_map(
        functools.partial(body, parts), mesh=mesh, in_specs=in_specs, out_specs=out_specs, check_vma=False
    )
```

```python
import functools

import jax
import jax.numpy as jnp
from jax import lax
from jax.experimental import pallas as pl
from jax.experimental.pallas import tpu as pltpu
from jax.sharding import PartitionSpec as P

BETA = 0.9
EPS = 1e-06
MIB = 1 << 20
ANY = pl.BlockSpec(memory_space=pl.ANY)


def for_slots(slots, assign_ref, count_ref, visit):
    owners = count_ref.shape[0]

    def one(o, offset):
        count = count_ref[o]
        for k, s in enumerate(slots):
            @pl.when(s < count)
            def _(k=k, s=s):
                visit(k * owners + o, assign_ref[offset + s], k, o)
        return offset + count

    lax.fori_loop(0, owners, one, 0)


def moment_kernel(slots, assign_ref, count_ref, *refs):
    grads, momentum = refs[:2]
    moment_out, outgoing, grad, old, new, half, in_sem, out_sem = refs[-8:]

    def reads(i, b):
        return (
            pltpu.make_async_copy(grads.at[b], grad.at[i], in_sem.at[0, i]),
            pltpu.make_async_copy(momentum.at[b], old.at[i], in_sem.at[1, i]),
        )

    def writes(i, b, k, o):
        return (
            pltpu.make_async_copy(half.at[i], outgoing.at[k, o], out_sem.at[0, i]),
            pltpu.make_async_copy(new.at[i], moment_out.at[b], out_sem.at[1, i]),
        )

    def start(i, b, k, o):
        for copy in reads(i, b):
            copy.start()

    def work(i, b, k, o):
        for copy in reads(i, b):
            copy.wait()
        moment = BETA * old[i] + (1.0 - BETA) * grad[i].astype(jnp.float32)
        new[i] = moment
        half[i] = moment.astype(jnp.bfloat16)
        for copy in writes(i, b, k, o):
            copy.start()

    def end(i, b, k, o):
        for copy in writes(i, b, k, o):
            copy.wait()

    for visit in (start, work, end):
        for_slots(slots, assign_ref, count_ref, visit)


def make_moment(slots, assign_list, owner_counts, grads, momentum, *earlier):
    blocks, rows, columns = grads.shape
    owners = owner_counts.shape[0]
    n = len(slots) * owners
    return pl.pallas_call(
        functools.partial(moment_kernel, slots),
        grid_spec=pltpu.PrefetchScalarGridSpec(
            num_scalar_prefetch=2,
            grid=(1,),
            in_specs=[ANY] * (2 + len(earlier)),
            out_specs=[ANY, ANY],
            scratch_shapes=[
                pltpu.VMEM((n, rows, columns), jnp.bfloat16),
                pltpu.VMEM((n, rows, columns), jnp.float32),
                pltpu.VMEM((n, rows, columns), jnp.float32),
                pltpu.VMEM((n, rows, columns), jnp.bfloat16),
                pltpu.SemaphoreType.DMA((2, n)),
                pltpu.SemaphoreType.DMA((2, n)),
            ],
        ),
        out_shape=[
            jax.ShapeDtypeStruct((blocks, rows, columns), jnp.float32),
            jax.ShapeDtypeStruct((len(slots), owners, rows, columns), jnp.bfloat16),
        ],
        input_output_aliases={4: 0} if earlier else {},
        compiler_params=pltpu.CompilerParams(vmem_limit_bytes=60 * MIB),
        cost_estimate=pl.CostEstimate(
            flops=3 * n * rows * columns, bytes_accessed=12 * n * rows * columns, transcendentals=0
        ),
    )(assign_list, owner_counts, grads, momentum, *earlier)


def finish_kernel(assign_ref, count_ref, scale_ref, *refs):
    arrived, update = refs[:-1], refs[-1]
    owners = count_ref.shape[0]

    def one(i, b, k, o):
        value = arrived[k][o].astype(jnp.float32) * scale_ref[k * owners + o]
        update[b] = value.astype(jnp.bfloat16)

    for_slots(range(len(arrived)), assign_ref, count_ref, one)


def finish(assign_list, owner_counts, scale, arrived):
    owners, rows, columns = arrived[0].shape
    blocks = assign_list.shape[0]
    full = pl.BlockSpec((owners, rows, columns), lambda i, *_: (0, 0, 0))
    return pl.pallas_call(
        finish_kernel,
        grid_spec=pltpu.PrefetchScalarGridSpec(
            num_scalar_prefetch=3,
            grid=(1,),
            in_specs=[full] * len(arrived),
            out_specs=pl.BlockSpec((blocks, rows, columns), lambda i, *_: (0, 0, 0)),
        ),
        out_shape=jax.ShapeDtypeStruct((blocks, rows, columns), jnp.bfloat16),
        compiler_params=pltpu.CompilerParams(vmem_limit_bytes=60 * MIB),
    )(assign_list, owner_counts, scale, *arrived)


def root_kernel(parts, count, turn_ref, *refs):
    moments, right, own_left, lefts = refs[:parts], refs[parts], refs[parts + 1], refs[parts + 2 : -3]
    out_ref, square_ref, product = refs[-3:]
    order, width = moments[0].shape
    step = min(256, order)
    turn = turn_ref[0]

    def position(d):
        return pl.multiple_of(lax.rem(turn - d + parts, parts) * width, width)

    def first(i, squares):
        rows = pl.ds(pl.multiple_of(i * step, step), step)
        total = None
        for d in range(parts):
            moment = moments[d][rows, :]
            term = lax.dot_general(
                moment,
                right[0, :, pl.ds(position(d), width)],
                (((1,), (1,)), ((), ())),
                preferred_element_type=jnp.float32,
            )
            total = term if total is None else total + term
            wide = moment.astype(jnp.float32)
            squares = squares + jnp.sum(wide * wide, axis=0, keepdims=True)
        product[rows, :] = total.astype(jnp.bfloat16)
        return squares

    zero = jnp.zeros((1, width), jnp.float32)
    moment_squares = lax.fori_loop(0, order // step, first, zero)
    squares = zero
    pieces = [(own_left.at[0], position(0))]
    for d in range(1, parts):
        base = position(d)
        for ref in lefts[(d - 1) * count : d * count]:
            pieces.append((ref, base))
            base = base + ref.shape[0]
    for left, base in pieces:
        height = left.shape[0]
        small = 256 if height % 256 == 0 else height
        for i in range(height // small):
            direction = jnp.dot(left[i * small : (i + 1) * small, :], product[...], preferred_element_type=jnp.float32)
            out_ref[pl.ds(pl.multiple_of(base + i * small, 16), small), :] = direction.astype(jnp.bfloat16)
            squares = squares + jnp.sum(direction * direction, axis=0, keepdims=True)
    for r, lines in enumerate((moment_squares, squares)):
        square_ref[r : r + 1, :] = jnp.broadcast_to(jnp.sum(lines, axis=1, keepdims=True), (1, 128))


def precondition(slot, turn, moments, right_root, left_root, lefts):
    parts = len(moments)
    order, width = moments[0].shape
    whole = pl.BlockSpec((order, width), lambda i, t: (0, 0))
    picked = pl.BlockSpec((1, width, order), lambda i, t: (slot, 0, 0))
    pieces = [piece for one in lefts for piece in one]
    return pl.pallas_call(
        functools.partial(root_kernel, parts, len(lefts[0])),
        grid_spec=pltpu.PrefetchScalarGridSpec(
            num_scalar_prefetch=1,
            grid=(1,),
            in_specs=[whole] * parts
            + [picked, picked]
            + [pl.BlockSpec((rows, order), lambda i, t, at=at: (at, 0)) for _, rows, at in pieces],
            out_specs=[whole, pl.BlockSpec((2, 128), lambda i, t: (0, 0))],
            scratch_shapes=[pltpu.VMEM((order, width), jnp.bfloat16)],
        ),
        out_shape=[
            jax.ShapeDtypeStruct((order, width), jnp.bfloat16),
            jax.ShapeDtypeStruct((2, 128), jnp.float32),
        ],
        compiler_params=pltpu.CompilerParams(vmem_limit_bytes=60 * MIB),
        cost_estimate=pl.CostEstimate(
            flops=4 * order * order * width, bytes_accessed=12 * order * width, transcendentals=0
        ),
    )(turn, *moments, right_root, left_root, *[x for x, _, _ in pieces])


def around(x, parts):
    return [
        lax.ppermute(x, "tensor", [(s, (s + d) % parts) for s in range(parts)]) for d in range(1, parts)
    ]


def all_sum(x, axis, size):
    stride = 1
    while stride < size:
        radix = min(4, size // stride)
        terms = [
            lax.ppermute(x, axis, [(s, s ^ (k * stride)) for s in range(size)]) for k in range(1, radix)
        ]
        x = sum(terms, x)
        stride *= radix
    return x


def after(x, *others):
    return lax.optimization_barrier((x, *others))[0]


def body(parts, grads, momentum, left_root, right_root, assign_list, owner_counts):
    cap, width, order = left_root.shape
    owners = owner_counts.shape[0]
    cells = float(order * order)
    turn = lax.axis_index("tensor").astype(jnp.int32).reshape(1)
    me = lax.axis_index("dp")

    def swap(x):
        return lax.all_to_all(x, "dp", split_axis=0, concat_axis=0, tiled=True)

    def solve(s, columns, others, lefts):
        direction, square = precondition(s, turn, [columns] + others, right_root, left_root, lefts)
        return direction.reshape(owners, order // owners, width), square[:, 0]

    unit = width // 4
    ahead = 9 * unit
    flat = left_root.reshape(cap * width, order)
    p0 = around(flat[:ahead], parts)
    moment_out, out0 = make_moment((0,), assign_list, owner_counts, grads, momentum)
    columns0 = swap(out0[0]).reshape(order, width)
    moment_out, rest = make_moment((1, 2), assign_list, owner_counts, grads, momentum, moment_out)
    m0 = around(columns0, parts)
    columns1 = swap(after(rest[0], columns0, *p0)).reshape(order, width)
    m1 = around(columns1, parts)
    columns2 = swap(after(rest[1], columns1, *m0)).reshape(order, width)
    d0, q0 = solve(0, columns0, m0, [[(p, width, 0)] for p in p0])
    m2 = around(columns2, parts)
    b0 = swap(after(d0, columns2, *m1))
    d1, q1 = solve(1, columns1, m1, [[(p, width, 1)] for p in p0])
    p1 = around(after(flat[ahead:], *m2), parts)
    b1 = swap(after(d1, b0, *m2))
    d2, q2 = solve(2, columns2, m2, [[(p, unit, 8), (q, 3 * unit, 0)] for p, q in zip(p0, p1)])
    b2 = swap(after(d2, b1))
    squares = jnp.stack([q0, q1, q2], axis=1)
    own = jnp.where(jnp.arange(owners)[None, None, :] == me, squares[:, :, None], 0.0)
    sums = all_sum(all_sum(own.reshape(2, -1), "tensor", parts), "dp", owners)
    scale = jnp.sqrt(sums[0] / (parts * cells) + EPS) / jnp.sqrt(sums[1] / cells + EPS)
    return (moment_out, finish(assign_list, owner_counts, scale, [b0, b1, b2]))


def solution(mesh):
    parts = mesh.shape["tensor"]
    in_specs = (
        P(None, "dp", "tensor"),
        P(None, "dp", "tensor"),
        P("dp", "tensor", None),
        P("dp", "tensor", None),
        P(),
        P(),
    )
    out_specs = (P(None, "dp", "tensor"), P(None, "dp", "tensor"))
    return jax.shard_map(
        functools.partial(body, parts), mesh=mesh, in_specs=in_specs, out_specs=out_specs, check_vma=False
    )
```

```python
import functools

import jax
import jax.numpy as jnp
from jax import lax
from jax.experimental import pallas as pl
from jax.experimental.pallas import tpu as pltpu
from jax.sharding import PartitionSpec as P

BETA = 0.9
EPS = 1e-06
MIB = 1 << 20
ANY = pl.BlockSpec(memory_space=pl.ANY)


def for_slots(slots, assign_ref, count_ref, visit):
    owners = count_ref.shape[0]

    def one(o, offset):
        count = count_ref[o]
        for k, s in enumerate(slots):
            @pl.when(s < count)
            def _(k=k, s=s):
                visit(k * owners + o, assign_ref[offset + s], k, o)
        return offset + count

    lax.fori_loop(0, owners, one, 0)


def moment_kernel(slots, assign_ref, count_ref, *refs):
    grads, momentum = refs[:2]
    moment_out, outgoing = refs[-7 - len(slots)], refs[-6 - len(slots) : -6]
    grad, old, new, half, in_sem, out_sem = refs[-6:]

    def reads(i, b):
        return (
            pltpu.make_async_copy(grads.at[b], grad.at[i], in_sem.at[0, i]),
            pltpu.make_async_copy(momentum.at[b], old.at[i], in_sem.at[1, i]),
        )

    def writes(i, b, k, o):
        return (
            pltpu.make_async_copy(half.at[i], outgoing[k].at[o], out_sem.at[0, i]),
            pltpu.make_async_copy(new.at[i], moment_out.at[b], out_sem.at[1, i]),
        )

    def start(i, b, k, o):
        for copy in reads(i, b):
            copy.start()

    def work(i, b, k, o):
        for copy in reads(i, b):
            copy.wait()
        moment = BETA * old[i] + (1.0 - BETA) * grad[i].astype(jnp.float32)
        new[i] = moment
        half[i] = moment.astype(jnp.bfloat16)
        for copy in writes(i, b, k, o):
            copy.start()

    def end(i, b, k, o):
        for copy in writes(i, b, k, o):
            copy.wait()

    for visit in (start, work, end):
        for_slots(slots, assign_ref, count_ref, visit)


def make_moment(slots, assign_list, owner_counts, grads, momentum, *earlier):
    blocks, rows, columns = grads.shape
    owners = owner_counts.shape[0]
    n = len(slots) * owners
    return pl.pallas_call(
        functools.partial(moment_kernel, slots),
        grid_spec=pltpu.PrefetchScalarGridSpec(
            num_scalar_prefetch=2,
            grid=(1,),
            in_specs=[ANY] * (2 + len(earlier)),
            out_specs=[ANY] * (1 + len(slots)),
            scratch_shapes=[
                pltpu.VMEM((n, rows, columns), jnp.bfloat16),
                pltpu.VMEM((n, rows, columns), jnp.float32),
                pltpu.VMEM((n, rows, columns), jnp.float32),
                pltpu.VMEM((n, rows, columns), jnp.bfloat16),
                pltpu.SemaphoreType.DMA((2, n)),
                pltpu.SemaphoreType.DMA((2, n)),
            ],
        ),
        out_shape=[
            jax.ShapeDtypeStruct((blocks, rows, columns), jnp.float32),
            *[jax.ShapeDtypeStruct((owners, rows, columns), jnp.bfloat16)] * len(slots),
        ],
        input_output_aliases={4: 0} if earlier else {},
        compiler_params=pltpu.CompilerParams(vmem_limit_bytes=60 * MIB),
        cost_estimate=pl.CostEstimate(
            flops=300 * n * rows * columns, bytes_accessed=1200 * n * rows * columns, transcendentals=0
        ),
    )(assign_list, owner_counts, grads, momentum, *earlier)


def place_kernel(slots, assign_ref, count_ref, *refs):
    arrived, update, sem = refs[: len(slots)], refs[-2], refs[-1]

    def copy(i, b, k, o):
        return pltpu.make_async_copy(arrived[k].at[o], update.at[b], sem.at[i])

    for_slots(slots, assign_ref, count_ref, lambda *at: copy(*at).start())
    for_slots(slots, assign_ref, count_ref, lambda *at: copy(*at).wait())


def place(slots, assign_list, owner_counts, arrived, *earlier):
    owners, rows, columns = arrived[0].shape
    return pl.pallas_call(
        functools.partial(place_kernel, slots),
        grid_spec=pltpu.PrefetchScalarGridSpec(
            num_scalar_prefetch=2,
            grid=(1,),
            in_specs=[pl.BlockSpec(memory_space=pltpu.VMEM)] * len(arrived) + [ANY] * len(earlier),
            out_specs=ANY,
            scratch_shapes=[pltpu.SemaphoreType.DMA((len(slots) * owners,))],
        ),
        out_shape=jax.ShapeDtypeStruct((assign_list.shape[0], rows, columns), jnp.bfloat16),
        input_output_aliases={2 + len(arrived): 0} if earlier else {},
        compiler_params=pltpu.CompilerParams(vmem_limit_bytes=8 * MIB),
        cost_estimate=pl.CostEstimate(
            flops=0, bytes_accessed=4 * len(slots) * owners * rows * columns, transcendentals=0
        ),
    )(assign_list, owner_counts, *arrived, *earlier)


def root_kernel(parts, count, turn_ref, *refs):
    moments, right, own_left, lefts = refs[:parts], refs[parts], refs[parts + 1], refs[parts + 2 : -4]
    out_ref, moment_square, square, product = refs[-4:]
    order, width = moments[0].shape
    step = min(256, order)
    turn = turn_ref[0]

    def position(d):
        return pl.multiple_of(lax.rem(turn - d + parts, parts) * width, width)

    def first(i, squares):
        rows = pl.ds(pl.multiple_of(i * step, step), step)
        total = None
        for d in range(parts):
            moment = moments[d][rows, :]
            term = lax.dot_general(
                moment,
                right[0, :, pl.ds(position(d), width)],
                (((1,), (1,)), ((), ())),
                preferred_element_type=jnp.float32,
            )
            total = term if total is None else total + term
            wide = moment.astype(jnp.float32)
            squares = squares + jnp.sum(wide * wide, axis=0, keepdims=True)
        product[rows, :] = total.astype(jnp.bfloat16)
        return squares

    zero = jnp.zeros((1, width), jnp.float32)
    moment_squares = lax.fori_loop(0, order // step, first, zero)
    squares = zero
    pieces = [(own_left.at[0], position(0))]
    for d in range(1, parts):
        base = position(d)
        for ref in lefts[(d - 1) * count : d * count]:
            pieces.append((ref, base))
            base = base + ref.shape[0]
    for left, base in pieces:
        height = left.shape[0]
        small = 256 if height % 256 == 0 else height
        for i in range(height // small):
            direction = jnp.dot(left[i * small : (i + 1) * small, :], product[...], preferred_element_type=jnp.float32)
            out_ref[pl.ds(pl.multiple_of(base + i * small, 16), small), :] = direction
            squares = squares + jnp.sum(direction * direction, axis=0, keepdims=True)
    for ref, lines in ((moment_square, moment_squares), (square, squares)):
        ref[...] = jnp.broadcast_to(jnp.sum(lines, axis=1, keepdims=True), (1, 128))


def precondition(slot, turn, moments, right_root, left_root, lefts):
    parts = len(moments)
    order, width = moments[0].shape
    whole = pl.BlockSpec((order, width), lambda i, t: (0, 0))
    picked = pl.BlockSpec((1, width, order), lambda i, t: (slot, 0, 0))
    pieces = [piece for one in lefts for piece in one]
    return pl.pallas_call(
        functools.partial(root_kernel, parts, len(lefts[0])),
        grid_spec=pltpu.PrefetchScalarGridSpec(
            num_scalar_prefetch=1,
            grid=(1,),
            in_specs=[whole] * parts
            + [picked, picked]
            + [pl.BlockSpec((rows, order), lambda i, t, at=at: (at, 0)) for _, rows, at in pieces],
            out_specs=[whole] + [pl.BlockSpec((1, 128), lambda i, t: (0, 0))] * 2,
            scratch_shapes=[pltpu.VMEM((order, width), jnp.bfloat16)],
        ),
        out_shape=[
            jax.ShapeDtypeStruct((order, width), jnp.float32),
            jax.ShapeDtypeStruct((1, 128), jnp.float32),
            jax.ShapeDtypeStruct((1, 128), jnp.float32),
        ],
        compiler_params=pltpu.CompilerParams(vmem_limit_bytes=60 * MIB),
        cost_estimate=pl.CostEstimate(
            flops=400 * order * order * width, bytes_accessed=1200 * order * width, transcendentals=0
        ),
    )(turn, *moments, right_root, left_root, *[x for x, _, _ in pieces])


def scale_kernel(cells, direction, moment_square, *refs):
    squares, out_ref = refs[:-1], refs[-1]
    total = sum([ref[0:1, 0:1] for ref in squares])
    scale = jnp.sqrt(moment_square[0:1, 0:1] / cells + EPS) / jnp.sqrt(total / cells + EPS)
    out_ref[...] = (direction[...] * scale).astype(jnp.bfloat16)


def rescale(direction, moment_square, squares):
    order, width = direction.shape
    return pl.pallas_call(
        functools.partial(scale_kernel, float(order * order)),
        out_shape=jax.ShapeDtypeStruct((order, width), jnp.bfloat16),
        compiler_params=pltpu.CompilerParams(vmem_limit_bytes=60 * MIB),
        cost_estimate=pl.CostEstimate(
            flops=order * width, bytes_accessed=6 * order * width, transcendentals=0
        ),
    )(direction, moment_square, *squares)


def around(x, parts):
    return [
        lax.ppermute(x, "tensor", [(s, (s + d) % parts) for s in range(parts)]) for d in range(1, parts)
    ]


def after(x, *others):
    return lax.optimization_barrier((x, *others))[0]


def gate(x, *others):
    return pl.pallas_call(
        lambda *refs: None,
        in_specs=[ANY] * (1 + len(others)),
        out_specs=ANY,
        out_shape=jax.ShapeDtypeStruct(x.shape, x.dtype),
        input_output_aliases={0: 0},
        compiler_params=pltpu.CompilerParams(vmem_limit_bytes=60 * MIB),
        cost_estimate=pl.CostEstimate(flops=1 << 37, bytes_accessed=1 << 28, transcendentals=0),
    )(x, *others)


def body(parts, grads, momentum, left_root, right_root, assign_list, owner_counts):
    cap, width, order = left_root.shape
    owners = owner_counts.shape[0]
    turn = lax.axis_index("tensor").astype(jnp.int32).reshape(1)

    def swap(x):
        return lax.all_to_all(x, "dp", split_axis=0, concat_axis=0, tiled=True)

    def solve(s, columns, others, lefts):
        direction, wanted, square = precondition(
            s, turn, [columns] + others, right_root, left_root, lefts
        )
        squares = [square] + around(square, parts)
        scaled = rescale(direction, wanted, squares)
        return scaled.reshape(owners, order // owners, width), squares[-1]

    unit = width // 4
    flat = left_root.reshape(cap * width, order)
    sent = []

    def send(first, end, *others):
        rows = flat[first * unit : end * unit]
        sent.append((first, end, around(after(rows, *others) if others else rows, parts)))
        return sent[-1][2]

    def lefts(s):
        pieces = [[] for _ in range(parts - 1)]
        for first, end, got in sent:
            low, high = max(first, 4 * s), min(end, 4 * s + 4)
            if low < high:
                for d, x in enumerate(got):
                    pieces[d].append((x, (high - low) * unit, (low - first) // (high - low)))
        return pieces

    p0 = send(0, 8)
    moment_out, out0 = make_moment((0,), assign_list, owner_counts, grads, momentum)
    columns0 = swap(out0).reshape(order, width)
    moment_out, out1, out2 = make_moment((1, 2), assign_list, owner_counts, grads, momentum, moment_out)
    m0 = around(columns0, parts)
    e1 = send(8, 9, columns0)
    columns1 = swap(gate(out1, columns0, *p0)).reshape(order, width)
    out2 = gate(out2, columns0)
    m1 = around(columns1, parts)
    e2 = []
    columns2 = swap(gate(out2, columns1, *m0, *e1)).reshape(order, width)
    d0, q0 = solve(0, columns0, m0, lefts(0))
    m2 = around(columns2, parts)
    e3 = []
    b0 = swap(gate(d0, columns2, *m1, *e2))
    d1, q1 = solve(1, columns1, m1, lefts(1))
    e4 = send(9, 12, q1)
    b1 = swap(gate(d1, b0, *m2))
    d2, q2 = solve(2, columns2, m2, lefts(2))
    b2 = swap(after(d2, b1))
    update = place((0, 1), assign_list, owner_counts, [b0, b1])
    update = place((2,), assign_list, owner_counts, [b2], update)
    return (moment_out, update)


def solution(mesh):
    parts = mesh.shape["tensor"]
    in_specs = (
        P(None, "dp", "tensor"),
        P(None, "dp", "tensor"),
        P("dp", "tensor", None),
        P("dp", "tensor", None),
        P(),
        P(),
    )
    out_specs = (P(None, "dp", "tensor"), P(None, "dp", "tensor"))
    return jax.shard_map(
        functools.partial(body, parts), mesh=mesh, in_specs=in_specs, out_specs=out_specs, check_vma=False
    )
```

```python
import functools

import jax
import jax.numpy as jnp
from jax import lax
from jax.experimental import pallas as pl
from jax.experimental.pallas import tpu as pltpu
from jax.sharding import PartitionSpec as P

BETA = 0.9
EPS = 1e-06
MIB = 1 << 20
ANY = pl.BlockSpec(memory_space=pl.ANY)


def for_slots(slots, assign_ref, count_ref, visit):
    owners = count_ref.shape[0]

    def one(o, offset):
        count = count_ref[o]
        for k, s in enumerate(slots):
            @pl.when(s < count)
            def _(k=k, s=s):
                visit(k * owners + o, assign_ref[offset + s], k, o)
        return offset + count

    lax.fori_loop(0, owners, one, 0)


def moment_kernel(slots, assign_ref, count_ref, *refs):
    grads, momentum = refs[:2]
    moment_out, outgoing = refs[-7 - len(slots)], refs[-6 - len(slots) : -6]
    grad, old, new, half, in_sem, out_sem = refs[-6:]

    def reads(i, b):
        return (
            pltpu.make_async_copy(grads.at[b], grad.at[i], in_sem.at[0, i]),
            pltpu.make_async_copy(momentum.at[b], old.at[i], in_sem.at[1, i]),
        )

    def writes(i, b, k, o):
        return (
            pltpu.make_async_copy(half.at[i], outgoing[k].at[o], out_sem.at[0, i]),
            pltpu.make_async_copy(new.at[i], moment_out.at[b], out_sem.at[1, i]),
        )

    def start(i, b, k, o):
        for copy in reads(i, b):
            copy.start()

    def work(i, b, k, o):
        for copy in reads(i, b):
            copy.wait()
        moment = BETA * old[i] + (1.0 - BETA) * grad[i].astype(jnp.float32)
        new[i] = moment
        half[i] = moment.astype(jnp.bfloat16)
        for copy in writes(i, b, k, o):
            copy.start()

    def end(i, b, k, o):
        for copy in writes(i, b, k, o):
            copy.wait()

    for visit in (start, work, end):
        for_slots(slots, assign_ref, count_ref, visit)


def make_moment(slots, assign_list, owner_counts, grads, momentum, *earlier):
    blocks, rows, columns = grads.shape
    owners = owner_counts.shape[0]
    n = len(slots) * owners
    return pl.pallas_call(
        functools.partial(moment_kernel, slots),
        grid_spec=pltpu.PrefetchScalarGridSpec(
            num_scalar_prefetch=2,
            grid=(1,),
            in_specs=[ANY] * (2 + len(earlier)),
            out_specs=[ANY] * (1 + len(slots)),
            scratch_shapes=[
                pltpu.VMEM((n, rows, columns), jnp.bfloat16),
                pltpu.VMEM((n, rows, columns), jnp.float32),
                pltpu.VMEM((n, rows, columns), jnp.float32),
                pltpu.VMEM((n, rows, columns), jnp.bfloat16),
                pltpu.SemaphoreType.DMA((2, n)),
                pltpu.SemaphoreType.DMA((2, n)),
            ],
        ),
        out_shape=[
            jax.ShapeDtypeStruct((blocks, rows, columns), jnp.float32),
            *[jax.ShapeDtypeStruct((owners, rows, columns), jnp.bfloat16)] * len(slots),
        ],
        input_output_aliases={4: 0} if earlier else {},
        compiler_params=pltpu.CompilerParams(vmem_limit_bytes=60 * MIB),
        cost_estimate=pl.CostEstimate(
            flops=300 * n * rows * columns, bytes_accessed=1200 * n * rows * columns, transcendentals=0
        ),
    )(assign_list, owner_counts, grads, momentum, *earlier)


def place_kernel(slots, assign_ref, count_ref, *refs):
    arrived, update, sem = refs[: len(slots)], refs[-2], refs[-1]

    def copy(i, b, k, o):
        return pltpu.make_async_copy(arrived[k].at[o], update.at[b], sem.at[i])

    for_slots(slots, assign_ref, count_ref, lambda *at: copy(*at).start())
    for_slots(slots, assign_ref, count_ref, lambda *at: copy(*at).wait())


def place(slots, assign_list, owner_counts, arrived, *earlier):
    owners, rows, columns = arrived[0].shape
    return pl.pallas_call(
        functools.partial(place_kernel, slots),
        grid_spec=pltpu.PrefetchScalarGridSpec(
            num_scalar_prefetch=2,
            grid=(1,),
            in_specs=[pl.BlockSpec(memory_space=pltpu.VMEM)] * len(arrived) + [ANY] * len(earlier),
            out_specs=ANY,
            scratch_shapes=[pltpu.SemaphoreType.DMA((len(slots) * owners,))],
        ),
        out_shape=jax.ShapeDtypeStruct((assign_list.shape[0], rows, columns), jnp.bfloat16),
        input_output_aliases={2 + len(arrived): 0} if earlier else {},
        compiler_params=pltpu.CompilerParams(vmem_limit_bytes=8 * MIB),
        cost_estimate=pl.CostEstimate(
            flops=0, bytes_accessed=4 * len(slots) * owners * rows * columns, transcendentals=0
        ),
    )(assign_list, owner_counts, *arrived, *earlier)


def root_kernel(parts, count, turn_ref, *refs):
    moments, right, own_left, lefts = refs[:parts], refs[parts], refs[parts + 1], refs[parts + 2 : -4]
    out_ref, moment_square, square, product = refs[-4:]
    order, width = moments[0].shape
    step = min(256, order)
    turn = turn_ref[0]

    def position(d):
        return pl.multiple_of(lax.rem(turn - d + parts, parts) * width, width)

    def first(i, squares):
        rows = pl.ds(pl.multiple_of(i * step, step), step)
        total = None
        for d in range(parts):
            moment = moments[d][rows, :]
            term = lax.dot_general(
                moment,
                right[0, :, pl.ds(position(d), width)],
                (((1,), (1,)), ((), ())),
                preferred_element_type=jnp.float32,
            )
            total = term if total is None else total + term
            wide = moment.astype(jnp.float32)
            squares = squares + jnp.sum(wide * wide, axis=0, keepdims=True)
        product[rows, :] = total.astype(jnp.bfloat16)
        return squares

    zero = jnp.zeros((1, width), jnp.float32)
    moment_squares = lax.fori_loop(0, order // step, first, zero)
    squares = zero
    pieces = [(own_left.at[0], position(0))]
    for d in range(1, parts):
        base = position(d)
        for ref in lefts[(d - 1) * count : d * count]:
            pieces.append((ref, base))
            base = base + ref.shape[0]
    for left, base in pieces:
        height = left.shape[0]
        small = 256 if height % 256 == 0 else height
        for i in range(height // small):
            direction = jnp.dot(left[i * small : (i + 1) * small, :], product[...], preferred_element_type=jnp.float32)
            out_ref[pl.ds(pl.multiple_of(base + i * small, 16), small), :] = direction
            squares = squares + jnp.sum(direction * direction, axis=0, keepdims=True)
    for ref, lines in ((moment_square, moment_squares), (square, squares)):
        ref[...] = jnp.broadcast_to(jnp.sum(lines, axis=1, keepdims=True), (1, 128))


def precondition(slot, turn, moments, right_root, left_root, lefts):
    parts = len(moments)
    order, width = moments[0].shape
    whole = pl.BlockSpec((order, width), lambda i, t: (0, 0))
    picked = pl.BlockSpec((1, width, order), lambda i, t: (slot, 0, 0))
    pieces = [piece for one in lefts for piece in one]
    return pl.pallas_call(
        functools.partial(root_kernel, parts, len(lefts[0])),
        grid_spec=pltpu.PrefetchScalarGridSpec(
            num_scalar_prefetch=1,
            grid=(1,),
            in_specs=[whole] * parts
            + [picked, picked]
            + [pl.BlockSpec((rows, order), lambda i, t, at=at: (at, 0)) for _, rows, at in pieces],
            out_specs=[whole] + [pl.BlockSpec((1, 128), lambda i, t: (0, 0))] * 2,
            scratch_shapes=[pltpu.VMEM((order, width), jnp.bfloat16)],
        ),
        out_shape=[
            jax.ShapeDtypeStruct((order, width), jnp.float32),
            jax.ShapeDtypeStruct((1, 128), jnp.float32),
            jax.ShapeDtypeStruct((1, 128), jnp.float32),
        ],
        compiler_params=pltpu.CompilerParams(vmem_limit_bytes=60 * MIB),
        cost_estimate=pl.CostEstimate(
            flops=400 * order * order * width, bytes_accessed=1200 * order * width, transcendentals=0
        ),
    )(turn, *moments, right_root, left_root, *[x for x, _, _ in pieces])


def product_kernel(parts, rows, turn_ref, *refs):
    split = len(rows)
    moments, right, product, square = refs[:-3], refs[-3], refs[-2], refs[-1]
    owners, _, width = product.shape
    turn = turn_ref[0]
    squares = jnp.zeros((1, width), jnp.float32)
    row = 0
    for r, height in enumerate(rows):
        group = min(owners, max(1, 256 // height))

        def some_owners(i, squares, r=r, height=height, row=row, group=group):
            some = pl.ds(i * group, group)
            total = None
            for d in range(parts):
                moment = moments[d * split + r][some].reshape(group * height, width)
                at = pl.multiple_of(lax.rem(turn - d + parts, parts) * width, width)
                term = lax.dot_general(
                    moment,
                    right[0, :, pl.ds(at, width)],
                    (((1,), (1,)), ((), ())),
                    preferred_element_type=jnp.float32,
                )
                total = term if total is None else total + term
                wide = moment.astype(jnp.float32)
                squares = squares + jnp.sum(wide * wide, axis=0, keepdims=True)
            half = total.astype(jnp.bfloat16).reshape(group, height, width)
            product[some, row : row + height, :] = half
            return squares

        squares = lax.fori_loop(0, owners // group, some_owners, squares)
        row += height
    square[...] = jnp.broadcast_to(jnp.sum(squares, axis=1, keepdims=True), (1, 128))


def make_product(slot, turn, moments, right_root):
    parts = len(moments)
    owners = moments[0][0][0].shape[0]
    _, width, order = right_root.shape
    rows = tuple(piece[1] for piece in moments[0])
    shares = [piece for one in moments for piece in one]
    shape = (owners, order // owners, width)
    return pl.pallas_call(
        functools.partial(product_kernel, parts, rows),
        grid_spec=pltpu.PrefetchScalarGridSpec(
            num_scalar_prefetch=1,
            grid=(1,),
            in_specs=[pl.BlockSpec((owners, n, width), lambda i, t, at=at: (0, at, 0)) for _, n, at in shares]
            + [pl.BlockSpec((1, width, order), lambda i, t: (slot, 0, 0))],
            out_specs=[pl.BlockSpec(shape, lambda i, t: (0, 0, 0)), pl.BlockSpec((1, 128), lambda i, t: (0, 0))],
        ),
        out_shape=[jax.ShapeDtypeStruct(shape, jnp.bfloat16), jax.ShapeDtypeStruct((1, 128), jnp.float32)],
        compiler_params=pltpu.CompilerParams(vmem_limit_bytes=60 * MIB),
        cost_estimate=pl.CostEstimate(
            flops=400 * order * order * width, bytes_accessed=1200 * order * width, transcendentals=0
        ),
    )(turn, *[x for x, _, _ in shares], right_root)


def direction_kernel(parts, count, turn_ref, product, own_left, *refs):
    lefts, out_ref, square = refs[:-2], refs[-2], refs[-1]
    order, width = product.shape
    turn = turn_ref[0]

    def position(d):
        return pl.multiple_of(lax.rem(turn - d + parts, parts) * width, width)

    squares = jnp.zeros((1, width), jnp.float32)
    pieces = [(own_left.at[0], position(0))]
    for d in range(1, parts):
        base = position(d)
        for ref in lefts[(d - 1) * count : d * count]:
            pieces.append((ref, base))
            base = base + ref.shape[0]
    for left, base in pieces:
        height = left.shape[0]
        small = 256 if height % 256 == 0 else height
        for i in range(height // small):
            direction = jnp.dot(
                left[i * small : (i + 1) * small, :], product[...], preferred_element_type=jnp.float32
            )
            out_ref[pl.ds(pl.multiple_of(base + i * small, 16), small), :] = direction
            squares = squares + jnp.sum(direction * direction, axis=0, keepdims=True)
    square[...] = jnp.broadcast_to(jnp.sum(squares, axis=1, keepdims=True), (1, 128))


def make_direction(slot, turn, product, left_root, lefts):
    _, width, order = left_root.shape
    pieces = [piece for one in lefts for piece in one]
    whole = pl.BlockSpec((order, width), lambda i, t: (0, 0))
    return pl.pallas_call(
        functools.partial(direction_kernel, len(lefts) + 1, len(lefts[0])),
        grid_spec=pltpu.PrefetchScalarGridSpec(
            num_scalar_prefetch=1,
            grid=(1,),
            in_specs=[whole, pl.BlockSpec((1, width, order), lambda i, t: (slot, 0, 0))]
            + [pl.BlockSpec((n, order), lambda i, t, at=at: (at, 0)) for _, n, at in pieces],
            out_specs=[whole, pl.BlockSpec((1, 128), lambda i, t: (0, 0))],
        ),
        out_shape=[jax.ShapeDtypeStruct((order, width), jnp.float32), jax.ShapeDtypeStruct((1, 128), jnp.float32)],
        compiler_params=pltpu.CompilerParams(vmem_limit_bytes=60 * MIB),
        cost_estimate=pl.CostEstimate(
            flops=2 * order * order * width, bytes_accessed=6 * order * width, transcendentals=0
        ),
    )(turn, product.reshape(order, width), left_root, *[x for x, _, _ in pieces])


def scale_kernel(cells, direction, moment_square, *refs):
    squares, out_ref = refs[:-1], refs[-1]
    total = sum([ref[0:1, 0:1] for ref in squares])
    scale = jnp.sqrt(moment_square[0:1, 0:1] / cells + EPS) / jnp.sqrt(total / cells + EPS)
    out_ref[...] = (direction[...] * scale).astype(jnp.bfloat16)


def rescale(direction, moment_square, squares):
    order, width = direction.shape
    return pl.pallas_call(
        functools.partial(scale_kernel, float(order * order)),
        out_shape=jax.ShapeDtypeStruct((order, width), jnp.bfloat16),
        compiler_params=pltpu.CompilerParams(vmem_limit_bytes=60 * MIB),
        cost_estimate=pl.CostEstimate(
            flops=order * width, bytes_accessed=6 * order * width, transcendentals=0
        ),
    )(direction, moment_square, *squares)


def around(x, parts):
    return [
        lax.ppermute(x, "tensor", [(s, (s + d) % parts) for s in range(parts)]) for d in range(1, parts)
    ]


def after(x, *others):
    return lax.optimization_barrier((x, *others))[0]


def gate(x, *others):
    return pl.pallas_call(
        lambda *refs: None,
        in_specs=[ANY] * (1 + len(others)),
        out_specs=ANY,
        out_shape=jax.ShapeDtypeStruct(x.shape, x.dtype),
        input_output_aliases={0: 0},
        compiler_params=pltpu.CompilerParams(vmem_limit_bytes=60 * MIB),
        cost_estimate=pl.CostEstimate(flops=1 << 37, bytes_accessed=1 << 28, transcendentals=0),
    )(x, *others)


def body(parts, grads, momentum, left_root, right_root, assign_list, owner_counts):
    cap, width, order = left_root.shape
    owners = owner_counts.shape[0]
    turn = lax.axis_index("tensor").astype(jnp.int32).reshape(1)

    def swap(x):
        return lax.all_to_all(x, "dp", split_axis=0, concat_axis=0, tiled=True)

    def solve(s, columns, others, lefts, apart=False):
        if apart:
            shape = (owners, order // owners, width)
            moments = [[(x.reshape(shape), shape[1], 0)] for x in [columns] + others]
            product, wanted = make_product(s, turn, moments, right_root)
            direction, square = make_direction(s, turn, product, left_root, lefts)
        else:
            direction, wanted, square = precondition(
                s, turn, [columns] + others, right_root, left_root, lefts
            )
        squares = [square] + around(square, parts)
        scaled = rescale(direction, wanted, squares)
        return scaled.reshape(owners, order // owners, width), squares[-1]

    unit = width // 4
    flat = left_root.reshape(cap * width, order)
    sent = []

    def send(first, end, *others):
        rows = flat[first * unit : end * unit]
        sent.append((first, end, around(after(rows, *others) if others else rows, parts)))
        return sent[-1][2]

    def lefts(s):
        pieces = [[] for _ in range(parts - 1)]
        for first, end, got in sent:
            low, high = max(first, 4 * s), min(end, 4 * s + 4)
            if low < high:
                for d, x in enumerate(got):
                    pieces[d].append((x, (high - low) * unit, (low - first) // (high - low)))
        return pieces

    p0 = send(0, 6)
    moment_out, out0 = make_moment((0,), assign_list, owner_counts, grads, momentum)
    columns0 = swap(out0).reshape(order, width)
    moment_out, out1, out2 = make_moment((1, 2), assign_list, owner_counts, grads, momentum, moment_out)
    out1 = gate(out1, *p0)
    m0 = around(columns0, parts)
    e1 = send(6, 7, columns0)
    columns1 = swap(gate(out1, columns0)).reshape(order, width)
    out2 = gate(out2, *m0, *e1)
    m1 = around(columns1, parts)
    columns2 = swap(gate(out2, columns1)).reshape(order, width)
    d0, q0 = solve(0, columns0, m0, lefts(0))
    e2 = send(7, 8, q0)
    m2 = around(columns2, parts)
    e3 = []
    b0 = swap(gate(d0, columns2, *m1, *e2))
    d1, q1 = solve(1, columns1, m1, lefts(1))
    e4 = send(8, 12, q1)
    b1 = swap(gate(d1, b0, *m2))
    d2, q2 = solve(2, columns2, m2, lefts(2), apart=True)
    b2 = swap(after(d2, b1))
    update = place((0, 1), assign_list, owner_counts, [b0, b1])
    update = place((2,), assign_list, owner_counts, [b2], update)
    return (moment_out, update)


def solution(mesh):
    parts = mesh.shape["tensor"]
    in_specs = (
        P(None, "dp", "tensor"),
        P(None, "dp", "tensor"),
        P("dp", "tensor", None),
        P("dp", "tensor", None),
        P(),
        P(),
    )
    out_specs = (P(None, "dp", "tensor"), P(None, "dp", "tensor"))
    return jax.shard_map(
        functools.partial(body, parts), mesh=mesh, in_specs=in_specs, out_specs=out_specs, check_vma=False
    )
```

```python
import functools

import jax
import jax.numpy as jnp
from jax import lax
from jax.experimental import pallas as pl
from jax.experimental.pallas import tpu as pltpu
from jax.sharding import PartitionSpec as P

BETA = 0.9
EPS = 1e-06
MIB = 1 << 20
ANY = pl.BlockSpec(memory_space=pl.ANY)


def for_slots(slots, assign_ref, count_ref, visit):
    owners = count_ref.shape[0]

    def one(o, offset):
        count = count_ref[o]
        for k, s in enumerate(slots):
            @pl.when(s < count)
            def _(k=k, s=s):
                visit(k * owners + o, assign_ref[offset + s], k, o)
        return offset + count

    lax.fori_loop(0, owners, one, 0)


def moment_kernel(slots, assign_ref, count_ref, *refs):
    grads, momentum = refs[:2]
    moment_out, outgoing = refs[-7 - len(slots)], refs[-6 - len(slots) : -6]
    grad, old, new, half, in_sem, out_sem = refs[-6:]

    def reads(i, b):
        return (
            pltpu.make_async_copy(grads.at[b], grad.at[i], in_sem.at[0, i]),
            pltpu.make_async_copy(momentum.at[b], old.at[i], in_sem.at[1, i]),
        )

    def writes(i, b, k, o):
        return (
            pltpu.make_async_copy(half.at[i], outgoing[k].at[o], out_sem.at[0, i]),
            pltpu.make_async_copy(new.at[i], moment_out.at[b], out_sem.at[1, i]),
        )

    def start(i, b, k, o):
        for copy in reads(i, b):
            copy.start()

    def work(i, b, k, o):
        for copy in reads(i, b):
            copy.wait()
        moment = BETA * old[i] + (1.0 - BETA) * grad[i].astype(jnp.float32)
        new[i] = moment
        half[i] = moment.astype(jnp.bfloat16)
        for copy in writes(i, b, k, o):
            copy.start()

    def end(i, b, k, o):
        for copy in writes(i, b, k, o):
            copy.wait()

    for visit in (start, work, end):
        for_slots(slots, assign_ref, count_ref, visit)


def make_moment(slots, assign_list, owner_counts, grads, momentum, *earlier):
    blocks, rows, columns = grads.shape
    owners = owner_counts.shape[0]
    n = len(slots) * owners
    return pl.pallas_call(
        functools.partial(moment_kernel, slots),
        grid_spec=pltpu.PrefetchScalarGridSpec(
            num_scalar_prefetch=2,
            grid=(1,),
            in_specs=[ANY] * (2 + len(earlier)),
            out_specs=[ANY] * (1 + len(slots)),
            scratch_shapes=[
                pltpu.VMEM((n, rows, columns), jnp.bfloat16),
                pltpu.VMEM((n, rows, columns), jnp.float32),
                pltpu.VMEM((n, rows, columns), jnp.float32),
                pltpu.VMEM((n, rows, columns), jnp.bfloat16),
                pltpu.SemaphoreType.DMA((2, n)),
                pltpu.SemaphoreType.DMA((2, n)),
            ],
        ),
        out_shape=[
            jax.ShapeDtypeStruct((blocks, rows, columns), jnp.float32),
            *[jax.ShapeDtypeStruct((owners, rows, columns), jnp.bfloat16)] * len(slots),
        ],
        input_output_aliases={4: 0} if earlier else {},
        compiler_params=pltpu.CompilerParams(vmem_limit_bytes=60 * MIB),
        cost_estimate=pl.CostEstimate(
            flops=300 * n * rows * columns, bytes_accessed=1200 * n * rows * columns, transcendentals=0
        ),
    )(assign_list, owner_counts, grads, momentum, *earlier)


def place_kernel(slots, assign_ref, count_ref, *refs):
    arrived, update, sem = refs[: len(slots)], refs[-2], refs[-1]

    def copy(i, b, k, o):
        return pltpu.make_async_copy(arrived[k].at[o], update.at[b], sem.at[i])

    for_slots(slots, assign_ref, count_ref, lambda *at: copy(*at).start())
    for_slots(slots, assign_ref, count_ref, lambda *at: copy(*at).wait())


def place(slots, assign_list, owner_counts, arrived, *earlier):
    owners, rows, columns = arrived[0].shape
    return pl.pallas_call(
        functools.partial(place_kernel, slots),
        grid_spec=pltpu.PrefetchScalarGridSpec(
            num_scalar_prefetch=2,
            grid=(1,),
            in_specs=[pl.BlockSpec(memory_space=pltpu.VMEM)] * len(arrived) + [ANY] * len(earlier),
            out_specs=ANY,
            scratch_shapes=[pltpu.SemaphoreType.DMA((len(slots) * owners,))],
        ),
        out_shape=jax.ShapeDtypeStruct((assign_list.shape[0], rows, columns), jnp.bfloat16),
        input_output_aliases={2 + len(arrived): 0} if earlier else {},
        compiler_params=pltpu.CompilerParams(vmem_limit_bytes=8 * MIB),
        cost_estimate=pl.CostEstimate(
            flops=0, bytes_accessed=4 * len(slots) * owners * rows * columns, transcendentals=0
        ),
    )(assign_list, owner_counts, *arrived, *earlier)


def root_kernel(parts, count, turn_ref, *refs):
    moments, right, own_left, lefts = refs[:parts], refs[parts], refs[parts + 1], refs[parts + 2 : -4]
    out_ref, moment_square, square, product = refs[-4:]
    order, width = moments[0].shape
    step = min(256, order)
    turn = turn_ref[0]

    def position(d):
        return pl.multiple_of(lax.rem(turn - d + parts, parts) * width, width)

    def first(i, squares):
        rows = pl.ds(pl.multiple_of(i * step, step), step)
        total = None
        for d in range(parts):
            moment = moments[d][rows, :]
            term = lax.dot_general(
                moment,
                right[0, :, pl.ds(position(d), width)],
                (((1,), (1,)), ((), ())),
                preferred_element_type=jnp.float32,
            )
            total = term if total is None else total + term
            wide = moment.astype(jnp.float32)
            squares = squares + jnp.sum(wide * wide, axis=0, keepdims=True)
        product[rows, :] = total.astype(jnp.bfloat16)
        return squares

    zero = jnp.zeros((1, width), jnp.float32)
    moment_squares = lax.fori_loop(0, order // step, first, zero)
    squares = zero
    pieces = [(own_left.at[0], position(0))]
    for d in range(1, parts):
        base = position(d)
        for ref in lefts[(d - 1) * count : d * count]:
            pieces.append((ref, base))
            base = base + ref.shape[0]
    for left, base in pieces:
        height = left.shape[0]
        small = 256 if height % 256 == 0 else height
        for i in range(height // small):
            direction = jnp.dot(left[i * small : (i + 1) * small, :], product[...], preferred_element_type=jnp.float32)
            out_ref[pl.ds(pl.multiple_of(base + i * small, 16), small), :] = direction
            squares = squares + jnp.sum(direction * direction, axis=0, keepdims=True)
    for ref, lines in ((moment_square, moment_squares), (square, squares)):
        ref[...] = jnp.broadcast_to(jnp.sum(lines, axis=1, keepdims=True), (1, 128))


def precondition(slot, turn, moments, right_root, left_root, lefts):
    parts = len(moments)
    order, width = moments[0].shape
    whole = pl.BlockSpec((order, width), lambda i, t: (0, 0))
    picked = pl.BlockSpec((1, width, order), lambda i, t: (slot, 0, 0))
    pieces = [piece for one in lefts for piece in one]
    return pl.pallas_call(
        functools.partial(root_kernel, parts, len(lefts[0])),
        grid_spec=pltpu.PrefetchScalarGridSpec(
            num_scalar_prefetch=1,
            grid=(1,),
            in_specs=[whole] * parts
            + [picked, picked]
            + [pl.BlockSpec((rows, order), lambda i, t, at=at: (at, 0)) for _, rows, at in pieces],
            out_specs=[whole] + [pl.BlockSpec((1, 128), lambda i, t: (0, 0))] * 2,
            scratch_shapes=[pltpu.VMEM((order, width), jnp.bfloat16)],
        ),
        out_shape=[
            jax.ShapeDtypeStruct((order, width), jnp.float32),
            jax.ShapeDtypeStruct((1, 128), jnp.float32),
            jax.ShapeDtypeStruct((1, 128), jnp.float32),
        ],
        compiler_params=pltpu.CompilerParams(vmem_limit_bytes=60 * MIB),
        cost_estimate=pl.CostEstimate(
            flops=400 * order * order * width, bytes_accessed=1200 * order * width, transcendentals=0
        ),
    )(turn, *moments, right_root, left_root, *[x for x, _, _ in pieces])


def product_kernel(parts, rows, turn_ref, *refs):
    split = len(rows)
    moments, right, product, square = refs[:-3], refs[-3], refs[-2], refs[-1]
    owners, _, width = product.shape
    turn = turn_ref[0]
    squares = jnp.zeros((1, width), jnp.float32)
    row = 0
    for r, height in enumerate(rows):
        group = min(owners, max(1, 256 // height))

        def some_owners(i, squares, r=r, height=height, row=row, group=group):
            some = pl.ds(i * group, group)
            total = None
            for d in range(parts):
                moment = moments[d * split + r][some].reshape(group * height, width)
                at = pl.multiple_of(lax.rem(turn - d + parts, parts) * width, width)
                term = lax.dot_general(
                    moment,
                    right[0, :, pl.ds(at, width)],
                    (((1,), (1,)), ((), ())),
                    preferred_element_type=jnp.float32,
                )
                total = term if total is None else total + term
                wide = moment.astype(jnp.float32)
                squares = squares + jnp.sum(wide * wide, axis=0, keepdims=True)
            half = total.astype(jnp.bfloat16).reshape(group, height, width)
            product[some, row : row + height, :] = half
            return squares

        squares = lax.fori_loop(0, owners // group, some_owners, squares)
        row += height
    square[...] = jnp.broadcast_to(jnp.sum(squares, axis=1, keepdims=True), (1, 128))


def make_product(slot, turn, moments, right_root):
    parts = len(moments)
    owners = moments[0][0][0].shape[0]
    _, width, order = right_root.shape
    rows = tuple(piece[1] for piece in moments[0])
    shares = [piece for one in moments for piece in one]
    shape = (owners, order // owners, width)
    return pl.pallas_call(
        functools.partial(product_kernel, parts, rows),
        grid_spec=pltpu.PrefetchScalarGridSpec(
            num_scalar_prefetch=1,
            grid=(1,),
            in_specs=[pl.BlockSpec((owners, n, width), lambda i, t, at=at: (0, at, 0)) for _, n, at in shares]
            + [pl.BlockSpec((1, width, order), lambda i, t: (slot, 0, 0))],
            out_specs=[pl.BlockSpec(shape, lambda i, t: (0, 0, 0)), pl.BlockSpec((1, 128), lambda i, t: (0, 0))],
        ),
        out_shape=[jax.ShapeDtypeStruct(shape, jnp.bfloat16), jax.ShapeDtypeStruct((1, 128), jnp.float32)],
        compiler_params=pltpu.CompilerParams(vmem_limit_bytes=60 * MIB),
        cost_estimate=pl.CostEstimate(
            flops=400 * order * order * width, bytes_accessed=1200 * order * width, transcendentals=0
        ),
    )(turn, *[x for x, _, _ in shares], right_root)


def direction_kernel(parts, count, turn_ref, product, own_left, *refs):
    lefts, out_ref, square = refs[:-2], refs[-2], refs[-1]
    order, width = product.shape
    turn = turn_ref[0]

    def position(d):
        return pl.multiple_of(lax.rem(turn - d + parts, parts) * width, width)

    squares = jnp.zeros((1, width), jnp.float32)
    pieces = [(own_left.at[0], position(0))]
    for d in range(1, parts):
        base = position(d)
        for ref in lefts[(d - 1) * count : d * count]:
            pieces.append((ref, base))
            base = base + ref.shape[0]
    for left, base in pieces:
        height = left.shape[0]
        small = 256 if height % 256 == 0 else height
        for i in range(height // small):
            direction = jnp.dot(
                left[i * small : (i + 1) * small, :], product[...], preferred_element_type=jnp.float32
            )
            out_ref[pl.ds(pl.multiple_of(base + i * small, 16), small), :] = direction
            squares = squares + jnp.sum(direction * direction, axis=0, keepdims=True)
    square[...] = jnp.broadcast_to(jnp.sum(squares, axis=1, keepdims=True), (1, 128))


def make_direction(slot, turn, product, left_root, lefts):
    _, width, order = left_root.shape
    pieces = [piece for one in lefts for piece in one]
    whole = pl.BlockSpec((order, width), lambda i, t: (0, 0))
    return pl.pallas_call(
        functools.partial(direction_kernel, len(lefts) + 1, len(lefts[0])),
        grid_spec=pltpu.PrefetchScalarGridSpec(
            num_scalar_prefetch=1,
            grid=(1,),
            in_specs=[whole, pl.BlockSpec((1, width, order), lambda i, t: (slot, 0, 0))]
            + [pl.BlockSpec((n, order), lambda i, t, at=at: (at, 0)) for _, n, at in pieces],
            out_specs=[pl.BlockSpec(memory_space=pltpu.VMEM)] * 2,
        ),
        out_shape=[jax.ShapeDtypeStruct((order, width), jnp.float32), jax.ShapeDtypeStruct((1, 128), jnp.float32)],
        compiler_params=pltpu.CompilerParams(vmem_limit_bytes=40 * MIB),
        cost_estimate=pl.CostEstimate(
            flops=2 * order * order * width, bytes_accessed=6 * order * width, transcendentals=0
        ),
    )(turn, product.reshape(order, width), left_root, *[x for x, _, _ in pieces])


def scale_kernel(cells, direction, moment_square, *refs):
    squares, out_ref = refs[:-1], refs[-1]
    total = sum([ref[0:1, 0:1] for ref in squares])
    scale = jnp.sqrt(moment_square[0:1, 0:1] / cells + EPS) / jnp.sqrt(total / cells + EPS)
    out_ref[...] = (direction[...] * scale).astype(jnp.bfloat16)


def rescale(direction, moment_square, squares, near):
    order, width = direction.shape
    vmem = pl.BlockSpec(memory_space=pltpu.VMEM)
    whole = pl.BlockSpec((order, width), lambda: (0, 0))
    return pl.pallas_call(
        functools.partial(scale_kernel, float(order * order)),
        in_specs=[vmem if near else whole] + [vmem] * (1 + len(squares)),
        out_specs=whole,
        out_shape=jax.ShapeDtypeStruct((order, width), jnp.bfloat16),
        compiler_params=pltpu.CompilerParams(vmem_limit_bytes=(32 if near else 60) * MIB),
        cost_estimate=pl.CostEstimate(
            flops=order * width, bytes_accessed=6 * order * width, transcendentals=0
        ),
    )(direction, moment_square, *squares)


def around(x, parts):
    return [
        lax.ppermute(x, "tensor", [(s, (s + d) % parts) for s in range(parts)]) for d in range(1, parts)
    ]


def after(x, *others):
    return lax.optimization_barrier((x, *others))[0]


def gate(x, *others):
    return pl.pallas_call(
        lambda *refs: None,
        in_specs=[ANY] * (1 + len(others)),
        out_specs=ANY,
        out_shape=jax.ShapeDtypeStruct(x.shape, x.dtype),
        input_output_aliases={0: 0},
        compiler_params=pltpu.CompilerParams(vmem_limit_bytes=60 * MIB),
        cost_estimate=pl.CostEstimate(flops=1 << 37, bytes_accessed=1 << 28, transcendentals=0),
    )(x, *others)


def body(parts, grads, momentum, left_root, right_root, assign_list, owner_counts):
    cap, width, order = left_root.shape
    owners = owner_counts.shape[0]
    turn = lax.axis_index("tensor").astype(jnp.int32).reshape(1)

    def swap(x):
        return lax.all_to_all(x, "dp", split_axis=0, concat_axis=0, tiled=True)

    def solve(s, columns, others, lefts, apart=False):
        if apart:
            shape = (owners, order // owners, width)
            moments = [[(x.reshape(shape), shape[1], 0)] for x in [columns] + others]
            product, wanted = make_product(s, turn, moments, right_root)
            direction, square = make_direction(s, turn, product, left_root, lefts)
        else:
            direction, wanted, square = precondition(
                s, turn, [columns] + others, right_root, left_root, lefts
            )
        squares = [square] + around(square, parts)
        scaled = rescale(direction, wanted, squares, apart)
        return scaled.reshape(owners, order // owners, width), squares[-1]

    unit = width // 4
    flat = left_root.reshape(cap * width, order)
    sent = []

    def send(first, end, *others):
        rows = flat[first * unit : end * unit]
        sent.append((first, end, around(after(rows, *others) if others else rows, parts)))
        return sent[-1][2]

    def lefts(s):
        pieces = [[] for _ in range(parts - 1)]
        for first, end, got in sent:
            low, high = max(first, 4 * s), min(end, 4 * s + 4)
            if low < high:
                for d, x in enumerate(got):
                    pieces[d].append((x, (high - low) * unit, (low - first) // (high - low)))
        return pieces

    p0 = send(0, 6)
    moment_out, out0 = make_moment((0,), assign_list, owner_counts, grads, momentum)
    columns0 = swap(out0).reshape(order, width)
    moment_out, out1, out2 = make_moment((1, 2), assign_list, owner_counts, grads, momentum, moment_out)
    out1 = gate(out1, *p0)
    m0 = around(columns0, parts)
    e1 = send(6, 7, columns0)
    columns1 = swap(gate(out1, columns0)).reshape(order, width)
    out2 = gate(out2, *m0, *e1)
    m1 = around(columns1, parts)
    columns2 = swap(gate(out2, columns1)).reshape(order, width)
    d0, q0 = solve(0, columns0, m0, lefts(0))
    e2 = send(7, 8, q0)
    m2 = around(columns2, parts)
    e3 = []
    b0 = swap(gate(d0, columns2, *m1))
    d1, q1 = solve(1, columns1, m1, lefts(1))
    e4 = send(8, 12, q1)
    b1 = swap(gate(d1, b0, *m2))
    d2, q2 = solve(2, columns2, m2, lefts(2), apart=True)
    b2 = swap(after(d2, b1))
    update = place((0, 1), assign_list, owner_counts, [b0, b1])
    update = place((2,), assign_list, owner_counts, [b2], update)
    return (moment_out, update)


def solution(mesh):
    parts = mesh.shape["tensor"]
    in_specs = (
        P(None, "dp", "tensor"),
        P(None, "dp", "tensor"),
        P("dp", "tensor", None),
        P("dp", "tensor", None),
        P(),
        P(),
    )
    out_specs = (P(None, "dp", "tensor"), P(None, "dp", "tensor"))
    return jax.shard_map(
        functools.partial(body, parts), mesh=mesh, in_specs=in_specs, out_specs=out_specs, check_vma=False
    )
```

```python
import functools

import jax
import jax.numpy as jnp
from jax import lax
from jax.experimental import pallas as pl
from jax.experimental.pallas import tpu as pltpu
from jax.sharding import PartitionSpec as P

BETA = 0.9
EPS = 1e-06
MIB = 1 << 20
ANY = pl.BlockSpec(memory_space=pl.ANY)


def for_slots(slots, assign_ref, count_ref, visit):
    owners = count_ref.shape[0]

    def one(o, offset):
        count = count_ref[o]
        for k, s in enumerate(slots):
            @pl.when(s < count)
            def _(k=k, s=s):
                visit(k * owners + o, assign_ref[offset + s], k, o)
        return offset + count

    lax.fori_loop(0, owners, one, 0)


def moment_kernel(slots, assign_ref, count_ref, *refs):
    grads, momentum = refs[:2]
    moment_out, outgoing = refs[-7 - len(slots)], refs[-6 - len(slots) : -6]
    grad, old, new, half, in_sem, out_sem = refs[-6:]

    def reads(i, b):
        return (
            pltpu.make_async_copy(grads.at[b], grad.at[i], in_sem.at[0, i]),
            pltpu.make_async_copy(momentum.at[b], old.at[i], in_sem.at[1, i]),
        )

    def writes(i, b, k, o):
        return (
            pltpu.make_async_copy(half.at[i], outgoing[k].at[o], out_sem.at[0, i]),
            pltpu.make_async_copy(new.at[i], moment_out.at[b], out_sem.at[1, i]),
        )

    def start(i, b, k, o):
        for copy in reads(i, b):
            copy.start()

    def work(i, b, k, o):
        for copy in reads(i, b):
            copy.wait()
        moment = BETA * old[i] + (1.0 - BETA) * grad[i].astype(jnp.float32)
        new[i] = moment
        half[i] = moment.astype(jnp.bfloat16)
        for copy in writes(i, b, k, o):
            copy.start()

    def end(i, b, k, o):
        for copy in writes(i, b, k, o):
            copy.wait()

    for visit in (start, work, end):
        for_slots(slots, assign_ref, count_ref, visit)


def make_moment(slots, assign_list, owner_counts, grads, momentum, *earlier):
    blocks, rows, columns = grads.shape
    owners = owner_counts.shape[0]
    n = len(slots) * owners
    return pl.pallas_call(
        functools.partial(moment_kernel, slots),
        grid_spec=pltpu.PrefetchScalarGridSpec(
            num_scalar_prefetch=2,
            grid=(1,),
            in_specs=[ANY] * (2 + len(earlier)),
            out_specs=[ANY] * (1 + len(slots)),
            scratch_shapes=[
                pltpu.VMEM((n, rows, columns), jnp.bfloat16),
                pltpu.VMEM((n, rows, columns), jnp.float32),
                pltpu.VMEM((n, rows, columns), jnp.float32),
                pltpu.VMEM((n, rows, columns), jnp.bfloat16),
                pltpu.SemaphoreType.DMA((2, n)),
                pltpu.SemaphoreType.DMA((2, n)),
            ],
        ),
        out_shape=[
            jax.ShapeDtypeStruct((blocks, rows, columns), jnp.float32),
            *[jax.ShapeDtypeStruct((owners, rows, columns), jnp.bfloat16)] * len(slots),
        ],
        input_output_aliases={4: 0} if earlier else {},
        compiler_params=pltpu.CompilerParams(vmem_limit_bytes=60 * MIB),
        cost_estimate=pl.CostEstimate(
            flops=300 * n * rows * columns, bytes_accessed=1200 * n * rows * columns, transcendentals=0
        ),
    )(assign_list, owner_counts, grads, momentum, *earlier)


def place_kernel(slots, assign_ref, count_ref, *refs):
    arrived, update, sem = refs[: len(slots)], refs[-2], refs[-1]

    def copy(i, b, k, o):
        return pltpu.make_async_copy(arrived[k].at[o], update.at[b], sem.at[i])

    for_slots(slots, assign_ref, count_ref, lambda *at: copy(*at).start())
    for_slots(slots, assign_ref, count_ref, lambda *at: copy(*at).wait())


def place(slots, assign_list, owner_counts, arrived, *earlier):
    owners, rows, columns = arrived[0].shape
    return pl.pallas_call(
        functools.partial(place_kernel, slots),
        grid_spec=pltpu.PrefetchScalarGridSpec(
            num_scalar_prefetch=2,
            grid=(1,),
            in_specs=[pl.BlockSpec(memory_space=pltpu.VMEM)] * len(arrived) + [ANY] * len(earlier),
            out_specs=ANY,
            scratch_shapes=[pltpu.SemaphoreType.DMA((len(slots) * owners,))],
        ),
        out_shape=jax.ShapeDtypeStruct((assign_list.shape[0], rows, columns), jnp.bfloat16),
        input_output_aliases={2 + len(arrived): 0} if earlier else {},
        compiler_params=pltpu.CompilerParams(vmem_limit_bytes=8 * MIB),
        cost_estimate=pl.CostEstimate(
            flops=0, bytes_accessed=4 * len(slots) * owners * rows * columns, transcendentals=0
        ),
    )(assign_list, owner_counts, *arrived, *earlier)


def root_kernel(parts, count, turn_ref, *refs):
    moments, right, own_left, lefts = refs[:parts], refs[parts], refs[parts + 1], refs[parts + 2 : -4]
    out_ref, moment_square, square, product = refs[-4:]
    order, width = moments[0].shape
    step = min(256, order)
    turn = turn_ref[0]

    def position(d):
        return pl.multiple_of(lax.rem(turn - d + parts, parts) * width, width)

    def first(i, squares):
        rows = pl.ds(pl.multiple_of(i * step, step), step)
        total = None
        for d in range(parts):
            moment = moments[d][rows, :]
            term = lax.dot_general(
                moment,
                right[0, :, pl.ds(position(d), width)],
                (((1,), (1,)), ((), ())),
                preferred_element_type=jnp.float32,
            )
            total = term if total is None else total + term
            wide = moment.astype(jnp.float32)
            squares = squares + jnp.sum(wide * wide, axis=0, keepdims=True)
        product[rows, :] = total.astype(jnp.bfloat16)
        return squares

    zero = jnp.zeros((1, width), jnp.float32)
    moment_squares = lax.fori_loop(0, order // step, first, zero)
    squares = zero
    pieces = [(own_left.at[0], position(0))]
    for d in range(1, parts):
        base = position(d)
        for ref in lefts[(d - 1) * count : d * count]:
            pieces.append((ref, base))
            base = base + ref.shape[0]
    for left, base in pieces:
        height = left.shape[0]
        small = 256 if height % 256 == 0 else height
        for i in range(height // small):
            direction = jnp.dot(left[i * small : (i + 1) * small, :], product[...], preferred_element_type=jnp.float32)
            out_ref[pl.ds(pl.multiple_of(base + i * small, 16), small), :] = direction
            squares = squares + jnp.sum(direction * direction, axis=0, keepdims=True)
    for ref, lines in ((moment_square, moment_squares), (square, squares)):
        ref[...] = jnp.broadcast_to(jnp.sum(lines, axis=1, keepdims=True), (1, 128))


def precondition(slot, turn, moments, right_root, left_root, lefts):
    parts = len(moments)
    order, width = moments[0].shape
    whole = pl.BlockSpec((order, width), lambda i, t: (0, 0))
    picked = pl.BlockSpec((1, width, order), lambda i, t: (slot, 0, 0))
    pieces = [piece for one in lefts for piece in one]
    return pl.pallas_call(
        functools.partial(root_kernel, parts, len(lefts[0])),
        grid_spec=pltpu.PrefetchScalarGridSpec(
            num_scalar_prefetch=1,
            grid=(1,),
            in_specs=[whole] * parts
            + [picked, picked]
            + [pl.BlockSpec((rows, order), lambda i, t, at=at: (at, 0)) for _, rows, at in pieces],
            out_specs=[whole] + [pl.BlockSpec((1, 128), lambda i, t: (0, 0))] * 2,
            scratch_shapes=[pltpu.VMEM((order, width), jnp.bfloat16)],
        ),
        out_shape=[
            jax.ShapeDtypeStruct((order, width), jnp.float32),
            jax.ShapeDtypeStruct((1, 128), jnp.float32),
            jax.ShapeDtypeStruct((1, 128), jnp.float32),
        ],
        compiler_params=pltpu.CompilerParams(vmem_limit_bytes=60 * MIB),
        cost_estimate=pl.CostEstimate(
            flops=400 * order * order * width, bytes_accessed=1200 * order * width, transcendentals=0
        ),
    )(turn, *moments, right_root, left_root, *[x for x, _, _ in pieces])


def product_kernel(parts, rows, turn_ref, *refs):
    split = len(rows)
    moments, right, product, square = refs[:-3], refs[-3], refs[-2], refs[-1]
    owners, _, width = product.shape
    turn = turn_ref[0]
    squares = jnp.zeros((1, width), jnp.float32)
    row = 0
    for r, height in enumerate(rows):
        group = min(owners, max(1, 256 // height))

        def some_owners(i, squares, r=r, height=height, row=row, group=group):
            some = pl.ds(i * group, group)
            total = None
            for d in range(parts):
                moment = moments[d * split + r][some].reshape(group * height, width)
                at = pl.multiple_of(lax.rem(turn - d + parts, parts) * width, width)
                term = lax.dot_general(
                    moment,
                    right[0, :, pl.ds(at, width)],
                    (((1,), (1,)), ((), ())),
                    preferred_element_type=jnp.float32,
                )
                total = term if total is None else total + term
                wide = moment.astype(jnp.float32)
                squares = squares + jnp.sum(wide * wide, axis=0, keepdims=True)
            half = total.astype(jnp.bfloat16).reshape(group, height, width)
            product[some, row : row + height, :] = half
            return squares

        squares = lax.fori_loop(0, owners // group, some_owners, squares)
        row += height
    square[...] = jnp.broadcast_to(jnp.sum(squares, axis=1, keepdims=True), (1, 128))


def make_product(slot, turn, moments, right_root):
    parts = len(moments)
    owners = moments[0][0][0].shape[0]
    _, width, order = right_root.shape
    rows = tuple(piece[1] for piece in moments[0])
    shares = [piece for one in moments for piece in one]
    shape = (owners, order // owners, width)
    return pl.pallas_call(
        functools.partial(product_kernel, parts, rows),
        grid_spec=pltpu.PrefetchScalarGridSpec(
            num_scalar_prefetch=1,
            grid=(1,),
            in_specs=[pl.BlockSpec((owners, n, width), lambda i, t, at=at: (0, at, 0)) for _, n, at in shares]
            + [pl.BlockSpec((1, width, order), lambda i, t: (slot, 0, 0))],
            out_specs=[pl.BlockSpec(shape, lambda i, t: (0, 0, 0)), pl.BlockSpec((1, 128), lambda i, t: (0, 0))],
        ),
        out_shape=[jax.ShapeDtypeStruct(shape, jnp.bfloat16), jax.ShapeDtypeStruct((1, 128), jnp.float32)],
        compiler_params=pltpu.CompilerParams(vmem_limit_bytes=60 * MIB),
        cost_estimate=pl.CostEstimate(
            flops=400 * order * order * width, bytes_accessed=1200 * order * width, transcendentals=0
        ),
    )(turn, *[x for x, _, _ in shares], right_root)


def direction_kernel(parts, count, turn_ref, product, own_left, *refs):
    lefts, out_ref, square = refs[:-2], refs[-2], refs[-1]
    order, width = product.shape
    turn = turn_ref[0]

    def position(d):
        return pl.multiple_of(lax.rem(turn - d + parts, parts) * width, width)

    squares = jnp.zeros((1, width), jnp.float32)
    pieces = [(own_left.at[0], position(0))]
    for d in range(1, parts):
        base = position(d)
        for ref in lefts[(d - 1) * count : d * count]:
            pieces.append((ref, base))
            base = base + ref.shape[0]
    for left, base in pieces:
        height = left.shape[0]
        small = 256 if height % 256 == 0 else height
        for i in range(height // small):
            direction = jnp.dot(
                left[i * small : (i + 1) * small, :], product[...], preferred_element_type=jnp.float32
            )
            out_ref[pl.ds(pl.multiple_of(base + i * small, 16), small), :] = direction
            squares = squares + jnp.sum(direction * direction, axis=0, keepdims=True)
    square[...] = jnp.broadcast_to(jnp.sum(squares, axis=1, keepdims=True), (1, 128))


def make_direction(slot, turn, product, left_root, lefts):
    _, width, order = left_root.shape
    pieces = [piece for one in lefts for piece in one]
    whole = pl.BlockSpec((order, width), lambda i, t: (0, 0))
    return pl.pallas_call(
        functools.partial(direction_kernel, len(lefts) + 1, len(lefts[0])),
        grid_spec=pltpu.PrefetchScalarGridSpec(
            num_scalar_prefetch=1,
            grid=(1,),
            in_specs=[whole, pl.BlockSpec((1, width, order), lambda i, t: (slot, 0, 0))]
            + [pl.BlockSpec((n, order), lambda i, t, at=at: (at, 0)) for _, n, at in pieces],
            out_specs=[pl.BlockSpec(memory_space=pltpu.VMEM)] * 2,
        ),
        out_shape=[jax.ShapeDtypeStruct((order, width), jnp.float32), jax.ShapeDtypeStruct((1, 128), jnp.float32)],
        compiler_params=pltpu.CompilerParams(vmem_limit_bytes=40 * MIB),
        cost_estimate=pl.CostEstimate(
            flops=2 * order * order * width, bytes_accessed=6 * order * width, transcendentals=0
        ),
    )(turn, product.reshape(order, width), left_root, *[x for x, _, _ in pieces])


def scale_kernel(cells, direction, moment_square, *refs):
    squares, out_ref = refs[:-1], refs[-1]
    total = sum([ref[0:1, 0:1] for ref in squares])
    scale = jnp.sqrt(moment_square[0:1, 0:1] / cells + EPS) / jnp.sqrt(total / cells + EPS)
    out_ref[...] = (direction[...] * scale).astype(jnp.bfloat16)


def rescale(direction, moment_square, squares, near):
    order, width = direction.shape
    vmem = pl.BlockSpec(memory_space=pltpu.VMEM)
    whole = pl.BlockSpec((order, width), lambda: (0, 0))
    return pl.pallas_call(
        functools.partial(scale_kernel, float(order * order)),
        in_specs=[vmem if near else whole] + [vmem] * (1 + len(squares)),
        out_specs=whole,
        out_shape=jax.ShapeDtypeStruct((order, width), jnp.bfloat16),
        compiler_params=pltpu.CompilerParams(vmem_limit_bytes=(32 if near else 60) * MIB),
        cost_estimate=pl.CostEstimate(
            flops=order * width, bytes_accessed=6 * order * width, transcendentals=0
        ),
    )(direction, moment_square, *squares)


def around(x, parts):
    return [
        lax.ppermute(x, "tensor", [(s, (s + d) % parts) for s in range(parts)]) for d in range(1, parts)
    ]


def after(x, *others):
    return lax.optimization_barrier((x, *others))[0]


def gate(x, *others):
    return pl.pallas_call(
        lambda *refs: None,
        in_specs=[ANY] * (1 + len(others)),
        out_specs=ANY,
        out_shape=jax.ShapeDtypeStruct(x.shape, x.dtype),
        input_output_aliases={0: 0},
        compiler_params=pltpu.CompilerParams(vmem_limit_bytes=60 * MIB),
        cost_estimate=pl.CostEstimate(flops=1 << 37, bytes_accessed=1 << 28, transcendentals=0),
    )(x, *others)


def body(parts, grads, momentum, left_root, right_root, assign_list, owner_counts):
    cap, width, order = left_root.shape
    owners = owner_counts.shape[0]
    turn = lax.axis_index("tensor").astype(jnp.int32).reshape(1)

    def swap(x):
        return lax.all_to_all(x, "dp", split_axis=0, concat_axis=0, tiled=True)

    def solve(s, columns, others, lefts, apart=False):
        if apart:
            shape = (owners, order // owners, width)
            moments = [[(x.reshape(shape), shape[1], 0)] for x in [columns] + others]
            product, wanted = make_product(s, turn, moments, right_root)
            direction, square = make_direction(s, turn, product, left_root, lefts)
        else:
            direction, wanted, square = precondition(
                s, turn, [columns] + others, right_root, left_root, lefts
            )
        squares = [square] + around(square, parts)
        scaled = rescale(direction, wanted, squares, apart)
        return scaled.reshape(owners, order // owners, width), squares[-1]

    unit = width // 4
    flat = left_root.reshape(cap * width, order)
    sent = []

    def send(first, end, *others):
        rows = flat[first * unit : end * unit]
        sent.append((first, end, around(after(rows, *others) if others else rows, parts)))
        return sent[-1][2]

    def lefts(s):
        pieces = [[] for _ in range(parts - 1)]
        for first, end, got in sent:
            low, high = max(first, 4 * s), min(end, 4 * s + 4)
            if low < high:
                for d, x in enumerate(got):
                    pieces[d].append((x, (high - low) * unit, (low - first) // (high - low)))
        return pieces

    p0 = send(0, 6)
    moment_out, out0 = make_moment((0,), assign_list, owner_counts, grads, momentum)
    columns0 = swap(out0).reshape(order, width)
    moment_out, out1, out2 = make_moment((1, 2), assign_list, owner_counts, grads, momentum, moment_out)
    out1 = gate(out1, *p0)
    m0 = around(columns0, parts)
    e1 = send(6, 7, columns0)
    columns1 = swap(gate(out1, columns0)).reshape(order, width)
    out2 = gate(out2, *m0)
    m1 = around(columns1, parts)
    columns2 = swap(gate(out2, columns1)).reshape(order, width)
    d0, q0 = solve(0, columns0, m0, lefts(0))
    e2 = send(7, 8, q0)
    m2 = around(columns2, parts)
    e3 = []
    b0 = swap(gate(d0, columns2, *m1, *e1))
    d1, q1 = solve(1, columns1, m1, lefts(1))
    e4 = send(8, 12, q1)
    b1 = swap(gate(d1, b0, *m2))
    d2, q2 = solve(2, columns2, m2, lefts(2), apart=True)
    b2 = swap(after(d2, b1))
    update = place((0, 1), assign_list, owner_counts, [b0, b1])
    update = place((2,), assign_list, owner_counts, [b2], update)
    return (moment_out, update)


def solution(mesh):
    parts = mesh.shape["tensor"]
    in_specs = (
        P(None, "dp", "tensor"),
        P(None, "dp", "tensor"),
        P("dp", "tensor", None),
        P("dp", "tensor", None),
        P(),
        P(),
    )
    out_specs = (P(None, "dp", "tensor"), P(None, "dp", "tensor"))
    return jax.shard_map(
        functools.partial(body, parts), mesh=mesh, in_specs=in_specs, out_specs=out_specs, check_vma=False
    )
```
